32 devices in a mesh: row: 4 (over y, x), col: 8 (over z, core).
Axes of the slice: x: 2, y: 2, z: 4, core: 2. Of those that a mesh axis runs over, the one named last changes fastest.
Arguments:
- ancestor_inverse: float32 [4096, 4096], P('row', 'col'), may hold values from -18 to 18, as said below
- panel: float32 [4096, 1024], P(('row', 'col')), may hold values from -0.09375 to 0.09375
- diag_inverse: float32 [1024, 1024], replicated, may hold values from -0.1875 to 0.1875
- inverse_pattern: int32 [16, 16], replicated, may hold values from 0 to 1, as said below
- panel_pattern: int32 [16, 4], replicated, may hold values 0 or 1
Outputs:
- sigma_panel: float32 [4096, 1024], P(('row', 'col'))
- sigma_diag: float32 [1024, 1024], replicated
The draws below stay inside these ranges and needn't reach their ends.
Inputs may be any that keep to these rules, and one draw needn't show every extreme that they name: `ancestor_inverse`: symmetric, so entry (i, j) equals entry (j, i). `inverse_pattern`: 1 marks a kept tile; the pattern is symmetric and every diagonal tile is kept. `panel_pattern`: 1 marks a nonzero tile.
All inputs are finite; a program needn't handle non-finite values.
Results may differ from the reference program's by a relative error of at most 0.000075.
Values sent between devices are 32-bit elements; how exact they have to be, the bound alone decides.
A program may use at most 128 MiB of HBM per device.

```python
import jax
import jax.numpy as jnp
from jax import lax

J = 1024
TILE = 256
S = 4096
N_COL = 8


def draw_ancestor_inverse(key, part):
    key = jax.random.fold_in(key, 5)
    base = jax.random.normal(key, (S, S), jnp.float32)
    paired = (base + base.T) * 0.70710678
    width = S // N_COL
    index_vals = jnp.arange(S, dtype=jnp.int32)
    same = index_vals[:, None] // width == index_vals[None, :] // width
    boosted = paired * jnp.where(same, 3.0, 1.0).astype(jnp.float32)
    return jnp.clip(boosted, -18.0, 18.0).astype(jnp.float32)


def draw_inverse_pattern(key, part):
    key = jax.random.fold_in(key, 11)
    tiles_count = S // TILE
    scores = jax.random.randint(key, (tiles_count, tiles_count), 0, 64)
    tile_rows = jnp.arange(tiles_count, dtype=jnp.int32)[:, None]
    tile_cols = jnp.arange(tiles_count, dtype=jnp.int32)[None, :]
    limits = 8 + 48 * tile_rows // max(tiles_count - 1, 1)
    keeper = (scores < limits) | (tile_rows == tile_cols)
    keeper = keeper | keeper.T
    return keeper.astype(jnp.int32)


def set_ends(result, own_key, low, top_value):
    index_at = [jax.random.randint(jax.random.fold_in(own_key, axis), (), 0, length) for axis, length in enumerate(result.shape)]
    main_axis = result.shape.index(max(result.shape))
    neighbour = index_at[:main_axis] + [(index_at[main_axis] + 1) % result.shape[main_axis]] + index_at[main_axis + 1:]
    return result.at[tuple(index_at)].set(low).at[tuple(neighbour)].set(top_value)


def steps_of(stream_key, dims, split, smallest, top_value):
    def one(dim, blocks):
        heights = jax.random.uniform(jax.random.fold_in(jax.random.fold_in(stream_key, 6), dim), (blocks,), jnp.float32, smallest / len(split), top_value / len(split))
        return jnp.repeat(jnp.exp(heights), dims[dim] // blocks).reshape((-1,) + (1,) * (len(dims) - dim - 1))

    factor_of = one(*split[0])
    for cut in split[1:]:
        factor_of = factor_of * one(*cut)
    return factor_of


def gaussian(own_key, dims, scale, limit, shards=(), held_as=jnp.bfloat16):
    values = jax.random.normal(own_key, dims, jnp.float32) * scale
    if len(shards) > 0:
        values = steps_of(own_key, dims, shards, -0.22, 0.18) * values
    return jnp.clip(values, min=-limit, max=limit).astype(held_as)


def setup_inputs(seed: int = 0) -> dict:
    streams_of = jax.random.split(jax.random.key(seed), 6)
    return {
        "ancestor_inverse": draw_ancestor_inverse(jax.random.fold_in(streams_of[5], 71), 0),
        "panel": gaussian(streams_of[1], (S, J), S ** -0.5, 0.09375, ((0, 32),), jnp.float32),
        "diag_inverse": gaussian(streams_of[2], (J, J), J ** -0.5, 0.1875, (), jnp.float32),
        "inverse_pattern": draw_inverse_pattern(jax.random.fold_in(streams_of[5], 71), 0),
        "panel_pattern": set_ends((jax.random.randint(streams_of[4], (S // TILE, J // TILE), 0, 3) < 2).astype(jnp.int32), jax.random.fold_in(streams_of[4], 1), 0, 1),
    }


HIGH = lax.Precision.HIGHEST


def reference(ancestor_inverse, panel, diag_inverse, inverse_pattern, panel_pattern):
    inv_factor = jnp.tril(diag_inverse) + jnp.eye(J, dtype=jnp.float32)
    panel_mask = jnp.repeat(jnp.repeat(panel_pattern.astype(jnp.float32), TILE, axis=0), TILE, axis=1)
    scaled_panel = jnp.dot(panel * panel_mask, inv_factor, precision=HIGH)
    blocks = ancestor_inverse.reshape(S // TILE, TILE, S)
    tile_flags = inverse_pattern.astype(jnp.float32)

    def one_block(pair):
        rows_block, flag_row = pair
        column_mask = jnp.repeat(flag_row, TILE)
        return -jnp.dot(rows_block * column_mask[None, :], scaled_panel, precision=HIGH)

    sigma_panel = lax.map(one_block, (blocks, tile_flags)).reshape(S, J)
    sigma_diag = jnp.dot(inv_factor.T, inv_factor, precision=HIGH) - jnp.dot(scaled_panel.T, sigma_panel, precision=HIGH)
    return sigma_panel, sigma_diag
```

```python
import jax
import jax.numpy as jnp
from jax import lax
from jax.sharding import PartitionSpec as P

TILE = 256


HIGH = lax.Precision.HIGH


def shards(ancestor_inverse, panel, diag_inverse, inverse_pattern, panel_pattern):
    rows_count = lax.axis_size("row")
    cols_count = lax.axis_size("col")
    row_at = lax.axis_index("row")
    col_at = lax.axis_index("col")
    block_rows, block_cols = ancestor_inverse.shape
    piece_rows, panel_width = panel.shape
    place = row_at * cols_count + col_at
    inv_factor = jnp.tril(diag_inverse) + jnp.eye(panel_width, dtype=jnp.float32)
    row_flags = lax.dynamic_slice_in_dim(panel_pattern, place * piece_rows // TILE, 1, 0).astype(jnp.float32)
    local_scaled = jnp.dot(panel * jnp.repeat(row_flags, TILE, axis=1), inv_factor, precision=HIGH)
    row_band = lax.all_gather(local_scaled, "col", axis=0, tiled=True)
    row_tiles = block_rows // TILE
    col_tiles = block_cols // TILE
    tile_flags = lax.dynamic_slice(
        inverse_pattern, (row_at * row_tiles, col_at * col_tiles), (row_tiles, col_tiles)
    )
    flag_values = tile_flags.astype(jnp.float32)
    masked_inverse = (
        ancestor_inverse.reshape(row_tiles, TILE, col_tiles, TILE) * flag_values[:, None, :, None]
    ).reshape(block_rows, block_cols)
    partial = -lax.dot_general(masked_inverse, row_band, (((0,), (0,)), ((), ())), precision=HIGH)
    summed = lax.psum_scatter(partial, "row", scatter_dimension=0, tiled=True)
    moves = [(r * cols_count + c, c * rows_count + r) for r in range(rows_count) for c in range(cols_count)]
    sigma_panel = lax.ppermute(summed, ("row", "col"), moves)
    share = panel_width // (rows_count * cols_count)
    factor_rows = lax.dynamic_slice_in_dim(inv_factor, place * share, share, 0)
    left = jnp.concatenate([local_scaled, factor_rows], axis=0)
    right = jnp.concatenate([-sigma_panel, factor_rows], axis=0)
    bands = []
    count = panel_width // TILE
    for i in range(count):
        part = lax.dot_general(
            left[:, i * TILE : (i + 1) * TILE], right[:, : (i + 1) * TILE], (((0,), (0,)), ((), ())), precision=HIGH
        )
        bands += [part[:, j * TILE : (j + 1) * TILE] for j in range(i + 1)]
    summed_tiles = lax.psum(jnp.concatenate(bands, axis=0), ("row", "col"))
    tile_at = lambda i, j: summed_tiles[(i * (i + 1) // 2 + j) * TILE :][:TILE]
    sigma_diag = jnp.concatenate(
        [
            jnp.concatenate([tile_at(i, j) if i >= j else tile_at(j, i).T for j in range(count)], axis=1)
            for i in range(count)
        ],
        axis=0,
    )
    return (sigma_panel, sigma_diag)


def solution(mesh):
    return jax.shard_map(
        shards,
        mesh=mesh,
        in_specs=(P("row", "col"), P(("row", "col"), None), P(), P(), P()),
        out_specs=(P(("row", "col"), None), P()),
        check_vma=False,
    )
```

```python
import functools

import jax
import jax.numpy as jnp
from jax import lax
from jax.experimental import pallas as pl
from jax.experimental.pallas import tpu as pltpu
from jax.sharding import PartitionSpec as P

TILE = 256
SHARE = 32


HIGH = lax.Precision.HIGH
MESH = pl.DeviceIdType.MESH


def halves(value):
    top = value.astype(jnp.bfloat16)
    return top, (value - top.astype(jnp.float32)).astype(jnp.bfloat16)


def product(left, right, dims):
    dot = lambda a, b: lax.dot_general(a, b, (dims, ((), ())), preferred_element_type=jnp.float32)
    return dot(left[0], right[0]) + (dot(left[0], right[1]) + dot(left[1], right[0]))


def body(
    chunk_rows, flags_ref, inv_ref, x_ref, f_ref, sigma_ref, diag_ref,
    at_high, at_low, l_high, l_low, band, partial, got_part, moved, raw,
    tiles, got_core, sums, got_row, got_line, whole,
    chain_send, chain_recv, swap_send, swap_recv, part_send, part_recv, move_send, move_recv,
    sum_send, core_recv, row_recv, line_recv, back_line, back_row, back_core,
):
    rows_n, cols_n = lax.axis_size("row"), lax.axis_size("col")
    line_n = cols_n // 2
    row, col = lax.axis_index("row"), lax.axis_index("col")
    line, core = col // 2, col % 2
    block_rows, block_cols = inv_ref.shape
    piece_rows, width = x_ref.shape
    count = width // TILE
    other_core = (row, 2 * line + 1 - core)
    row_peers = [((row + d) % rows_n, col) for d in range(1, rows_n)]
    line_peers = [(row, 2 * ((line + d) % line_n) + core) for d in range(1, line_n)]
    peers = [other_core] + row_peers + line_peers
    target_at = col * rows_n + row
    target = (target_at // cols_n, target_at % cols_n)
    own_at = row * cols_n + col
    source = (own_at % rows_n, own_at // rows_n)
    stays = target_at == own_at

    barrier = pltpu.get_barrier_semaphore()
    for peer in peers:
        pl.semaphore_signal(barrier, inc=1, device_id=peer, device_id_type=MESH)

    @pl.when(jnp.logical_not(stays))
    def _():
        pl.semaphore_signal(barrier, inc=1, device_id=source, device_id_type=MESH)

    for j in range(count):
        band[j, pl.ds(pl.multiple_of(col * piece_rows, 8), piece_rows)] = x_ref[:, j * TILE : (j + 1) * TILE]

    @pl.when(stays)
    def _():
        pl.semaphore_wait(barrier, len(peers))

    @pl.when(jnp.logical_not(stays))
    def _():
        pl.semaphore_wait(barrier, len(peers) + 1)

    def span(start, size):
        return pl.ds(pl.multiple_of(start, 8), size)

    def remote(src, dst, send_sem, recv_sem, peer):
        return pltpu.make_async_remote_copy(
            src_ref=src, dst_ref=dst, send_sem=send_sem, recv_sem=recv_sem, device_id=peer, device_id_type=MESH
        )

    def begin(src, dst, send_sem, recv_sem, peer):
        copy = remote(src, dst, send_sem, recv_sem, peer)
        copy.start()
        return copy

    def prepare():
        for a in range(block_rows // TILE):
            for b in range(block_cols // TILE):
                flag = flags_ref[row * (block_rows // TILE) + a, col * (block_cols // TILE) + b].astype(jnp.float32)
                tile = inv_ref[a * TILE : (a + 1) * TILE, b * TILE : (b + 1) * TILE] * flag
                top, rest = halves(tile.T)
                at_high[b * TILE : (b + 1) * TILE, a * TILE : (a + 1) * TILE] = top
                at_low[b * TILE : (b + 1) * TILE, a * TILE : (a + 1) * TILE] = rest
        top, rest = halves(jnp.concatenate([x_ref[...], f_ref[...]], axis=0))
        l_high[...] = top
        l_low[...] = rest

    def chunk(j):
        def piece_of(at, k):
            return band.at[j, span((2 * at + k) * piece_rows, piece_rows)]

        def hop(way, s):
            begun = line - way * (s - 1)
            came = line - way * s
            n = 0 if way > 0 else 1
            go = (line + way >= 0) & (line + way < line_n) & (begun >= 0) & (begun < line_n)
            arrives = (came >= 0) & (came < line_n)
            sem = (j, n, s)
            return go, arrives, begun, came, sem

        def hop_copy(at, sem, way):
            place = piece_of(at, core)
            return remote(place, place, chain_send.at[sem], chain_recv.at[sem], (row, 2 * (line + way) + core))

        def swap(at, slot):
            place = piece_of(at, core)
            return remote(place, place, swap_send.at[j, slot], swap_recv.at[j, slot], other_core)

        for s in range(1, line_n):
            for way in (1, -1):
                go, _, begun, _, sem = hop(way, s)

                @pl.when(go)
                def _():
                    hop_copy(begun, sem, way).start()

            if s == 1:
                swap(line, 0).start()
            yield
            for way in (1, -1):
                _, arrives, _, came, sem = hop(way, s)
                slot = 2 * s - 1 if way > 0 else 2 * s

                @pl.when(arrives)
                def _():
                    hop_copy(came, sem, way).wait_recv()
                    swap(came, slot).start()

        for s in range(1, line_n):
            for way in (1, -1):
                go, arrives, begun, came, sem = hop(way, s)
                slot = 2 * s - 1 if way > 0 else 2 * s

                @pl.when(go)
                def _():
                    hop_copy(begun, sem, way).wait_send()

                @pl.when(arrives)
                def _():
                    swap(came, slot).wait()

        swap(line, 0).wait()
        partial[j] = product((at_high[...], at_low[...]), halves(band[j]), ((1,), (0,)))
        copies = []
        for d in range(1, rows_n):
            to = (row + d) % rows_n
            src = partial.at[j, span(to * piece_rows, piece_rows)]
            copies.append(begin(src, got_part.at[j, d], part_send.at[j, d], part_recv.at[j, d], row_peers[d - 1]))
        yield
        for copy in copies:
            copy.wait()
        value = partial[j, span(row * piece_rows, piece_rows)]
        for d in range(1, rows_n):
            value = value + got_part[j, d]
        raw[j] = value
        move = lambda: remote(raw.at[j], moved.at[j], move_send.at[j], move_recv.at[j], target)

        @pl.when(jnp.logical_not(stays))
        def _():
            move().start()

        @pl.when(stays)
        def _():
            moved[j] = raw[j]

        yield

        @pl.when(jnp.logical_not(stays))
        def _():
            move().wait()

        here = slice(j * TILE, (j + 1) * TILE)
        sigma_ref[:, here] = -moved[j]
        full = (count - j) * TILE
        total = chunk_rows[j]
        base = sum(chunk_rows[:j])
        right = halves(jnp.concatenate([moved[j], f_ref[:, here]], axis=0))
        tiles[base : base + full] = product((l_high[:, j * TILE :], l_low[:, j * TILE :]), right, ((0,), (0,)))
        if total > full:
            tiles[base + full : base + total] = jnp.zeros((total - full, TILE), jnp.float32)
        half, part = total // 2, total // (2 * rows_n)
        piece = part // line_n
        base_half, base_part, base_piece = base // 2, base // (2 * rows_n), base // (2 * rows_n * line_n)
        src = tiles.at[span(base + (1 - core) * half, half)]
        copy = begin(src, got_core.at[base_half : base_half + half], sum_send.at[j, 0], core_recv.at[j], other_core)
        yield
        copy.wait()
        own = span(base + core * half, half)
        sums[base_half : base_half + half] = tiles[own] + got_core[base_half : base_half + half]
        here_part = slice(base_part, base_part + part)
        copies = []
        for d in range(1, rows_n):
            to = (row + d) % rows_n
            src = sums.at[span(base_half + to * part, part)]
            copies.append(
                begin(src, got_row.at[d, here_part], sum_send.at[j, d], row_recv.at[j, d], row_peers[d - 1])
            )
        yield
        for copy in copies:
            copy.wait()
        value = sums[span(base_half + row * part, part)]
        for d in range(1, rows_n):
            value = value + got_row[d, here_part]
        got_row[0, here_part] = value
        here_piece = slice(base_piece, base_piece + piece)
        copies = []
        for d in range(1, line_n):
            to = (line + d) % line_n
            src = got_row.at[0, span(base_part + to * piece, piece)]
            copies.append(
                begin(src, got_line.at[d, here_piece], sum_send.at[j, d], line_recv.at[j, d], line_peers[d - 1])
            )
        yield
        for copy in copies:
            copy.wait()
        value = got_row[0, span(base_part + line * piece, piece)]
        for d in range(1, line_n):
            value = value + got_line[d, here_piece]
        mine = span(base + core * half + row * part + line * piece, piece)
        whole[mine] = value
        copies = [
            begin(whole.at[mine], whole.at[mine], sum_send.at[j, d], back_line.at[j, d], line_peers[d - 1])
            for d in range(1, line_n)
        ]
        yield
        for copy in copies:
            copy.wait()
        mine = span(base + core * half + row * part, part)
        copies = [
            begin(whole.at[mine], whole.at[mine], sum_send.at[j, d], back_row.at[j, d], row_peers[d - 1])
            for d in range(1, rows_n)
        ]
        yield
        for copy in copies:
            copy.wait()
        mine = span(base + core * half, half)
        copy = begin(whole.at[mine], whole.at[mine], sum_send.at[j, 0], back_core.at[j], other_core)
        yield
        copy.wait()
        for i in range(j, count):
            tile = whole[base + (i - j) * TILE : base + (i - j + 1) * TILE]
            diag_ref[i * TILE : (i + 1) * TILE, here] = tile
            if i != j:
                diag_ref[here, i * TILE : (i + 1) * TILE] = tile.T

    waiting = [chunk(j) for j in range(count)]
    active = []
    first = True
    while waiting or active:
        if waiting:
            active.append(waiting.pop(0))
        active = [flow for flow in active if next(flow, "end") != "end"]
        if first:
            prepare()
            first = False


def finish(pattern, inverse, scaled, factor_rows):
    rows_n = lax.axis_size("row")
    cols_n = lax.axis_size("col")
    line_n = cols_n // 2
    piece_rows, width = scaled.shape
    block_rows, block_cols = inverse.shape
    count = width // TILE
    shares = 2 * rows_n * line_n
    chunk_rows = tuple(-(-(count - j) * TILE // (8 * shares)) * 8 * shares for j in range(count))
    total = sum(chunk_rows)
    most = max(rows_n, line_n)
    dma = pltpu.SemaphoreType.DMA
    vmem = pl.BlockSpec(memory_space=pltpu.VMEM)
    f32, b16 = jnp.float32, jnp.bfloat16
    return pl.pallas_call(
        functools.partial(body, chunk_rows),
        out_shape=(
            jax.ShapeDtypeStruct((piece_rows, width), f32),
            jax.ShapeDtypeStruct((width, width), f32),
        ),
        in_specs=[pl.BlockSpec(memory_space=pltpu.SMEM), vmem, vmem, vmem],
        out_specs=(vmem, vmem),
        scratch_shapes=[
            pltpu.VMEM((block_cols, block_rows), b16),
            pltpu.VMEM((block_cols, block_rows), b16),
            pltpu.VMEM((piece_rows + SHARE, width), b16),
            pltpu.VMEM((piece_rows + SHARE, width), b16),
            pltpu.VMEM((count, block_rows, TILE), f32),
            pltpu.VMEM((count, block_cols, TILE), f32),
            pltpu.VMEM((count, rows_n, piece_rows, TILE), f32),
            pltpu.VMEM((count, piece_rows, TILE), f32),
            pltpu.VMEM((count, piece_rows, TILE), f32),
            pltpu.VMEM((total, TILE), f32),
            pltpu.VMEM((total // 2, TILE), f32),
            pltpu.VMEM((total // 2, TILE), f32),
            pltpu.VMEM((rows_n, total // (2 * rows_n), TILE), f32),
            pltpu.VMEM((line_n, total // shares, TILE), f32),
            pltpu.VMEM((total, TILE), f32),
            dma((count, 2, line_n)),
            dma((count, 2, line_n)),
            dma((count, 2 * line_n)),
            dma((count, 2 * line_n)),
            dma((count, rows_n)),
            dma((count, rows_n)),
            dma((count,)),
            dma((count,)),
            dma((count, most)),
            dma((count,)),
            dma((count, rows_n)),
            dma((count, line_n)),
            dma((count, line_n)),
            dma((count, rows_n)),
            dma((count,)),
        ],
        compiler_params=pltpu.CompilerParams(collective_id=0, has_side_effects=True, vmem_limit_bytes=56 << 20),
    )(pattern, inverse, scaled, factor_rows)


def shards(ancestor_inverse, panel, diag_inverse, inverse_pattern, panel_pattern):
    rows_count = lax.axis_size("row")
    cols_count = lax.axis_size("col")
    piece_rows, panel_width = panel.shape
    place = lax.axis_index("row") * cols_count + lax.axis_index("col")
    inv_factor = jnp.tril(diag_inverse) + jnp.eye(panel_width, dtype=jnp.float32)
    row_flags = lax.dynamic_slice_in_dim(panel_pattern, place * piece_rows // TILE, 1, 0).astype(jnp.float32)
    local_scaled = jnp.dot(panel * jnp.repeat(row_flags, TILE, axis=1), inv_factor, precision=HIGH)
    share = panel_width // (rows_count * cols_count)
    factor_rows = lax.dynamic_slice_in_dim(inv_factor, place * share, share, 0)
    if share < SHARE:
        factor_rows = jnp.pad(factor_rows, ((0, SHARE - share), (0, 0)))
    return finish(inverse_pattern, ancestor_inverse, local_scaled, factor_rows)


def solution(mesh):
    return jax.shard_map(
        shards,
        mesh=mesh,
        in_specs=(P("row", "col"), P(("row", "col"), None), P(), P(), P()),
        out_specs=(P(("row", "col"), None), P()),
        check_vma=False,
    )
```

```python
import functools

import jax
import jax.numpy as jnp
from jax import lax
from jax.experimental import pallas as pl
from jax.experimental.pallas import tpu as pltpu
from jax.sharding import PartitionSpec as P

TILE = 256
SHARE = 32


MESH = pl.DeviceIdType.MESH


def halves(value):
    top = value.astype(jnp.bfloat16)
    return top, (value - top.astype(jnp.float32)).astype(jnp.bfloat16)


def product(left, right, dims):
    dot = lambda a, b: lax.dot_general(a, b, (dims, ((), ())), preferred_element_type=jnp.float32)
    return dot(left[0], right[0]) + (dot(left[0], right[1]) + dot(left[1], right[0]))


def body(
    chunk_rows, flags_ref, panel_flags_ref, inv_ref, panel_ref, factor_ref, moved, whole,
    at_high, at_low, p_high, p_low, l_high, l_low, f_ref, band, partial, got_part, raw,
    tiles, got_core, sums, got_row, got_line,
    chain_send, chain_recv, swap_send, swap_recv, part_send, part_recv, move_send, move_recv,
    sum_send, core_recv, row_recv, line_recv, back_line, back_row, back_core,
):
    rows_n, cols_n = lax.axis_size("row"), lax.axis_size("col")
    line_n = cols_n // 2
    row, col = lax.axis_index("row"), lax.axis_index("col")
    line, core = col // 2, col % 2
    block_rows, block_cols = inv_ref.shape
    piece_rows, width = panel_ref.shape
    count = width // TILE
    other_core = (row, 2 * line + 1 - core)
    row_peers = [((row + d) % rows_n, col) for d in range(1, rows_n)]
    line_peers = [(row, 2 * ((line + d) % line_n) + core) for d in range(1, line_n)]
    peers = [other_core] + row_peers + line_peers
    target_at = col * rows_n + row
    target = (target_at // cols_n, target_at % cols_n)
    own_at = row * cols_n + col
    source = (own_at % rows_n, own_at // rows_n)
    stays = target_at == own_at

    barrier = pltpu.get_barrier_semaphore()
    for peer in peers:
        pl.semaphore_signal(barrier, inc=1, device_id=peer, device_id_type=MESH)

    @pl.when(jnp.logical_not(stays))
    def _():
        pl.semaphore_signal(barrier, inc=1, device_id=source, device_id_type=MESH)

    share = width // (rows_n * cols_n)
    first = own_at * share
    start = first // SHARE * SHARE
    ids = start + lax.broadcasted_iota(jnp.int32, (SHARE, width), 0)
    places = lax.broadcasted_iota(jnp.int32, (SHARE, width), 1)
    rows = jnp.where(ids >= places, factor_ref[pl.ds(pl.multiple_of(start, 8), SHARE)], 0.0)
    rows = rows + jnp.where(ids == places, 1.0, 0.0)
    f_ref[...] = jnp.where((ids >= first) & (ids < first + share), rows, 0.0)
    for k in range(count):
        here = slice(k * TILE, (k + 1) * TILE)
        flag = panel_flags_ref[own_at * piece_rows // TILE, k].astype(jnp.float32)
        p_high[:, here], p_low[:, here] = halves(panel_ref[:, here] * flag)

    @pl.when(stays)
    def _():
        pl.semaphore_wait(barrier, len(peers))

    @pl.when(jnp.logical_not(stays))
    def _():
        pl.semaphore_wait(barrier, len(peers) + 1)

    def span(start, size):
        return pl.ds(pl.multiple_of(start, 8), size)

    def remote(src, dst, send_sem, recv_sem, peer):
        return pltpu.make_async_remote_copy(
            src_ref=src, dst_ref=dst, send_sem=send_sem, recv_sem=recv_sem, device_id=peer, device_id_type=MESH
        )

    def begin(src, dst, send_sem, recv_sem, peer):
        copy = remote(src, dst, send_sem, recv_sem, peer)
        copy.start()
        return copy

    def prepare():
        for a in range(block_rows // TILE):
            for b in range(block_cols // TILE):
                flag = flags_ref[row * (block_rows // TILE) + a, col * (block_cols // TILE) + b].astype(jnp.float32)
                tile = inv_ref[a * TILE : (a + 1) * TILE, b * TILE : (b + 1) * TILE] * flag
                top, rest = halves(tile.T)
                at_high[b * TILE : (b + 1) * TILE, a * TILE : (a + 1) * TILE] = top
                at_low[b * TILE : (b + 1) * TILE, a * TILE : (a + 1) * TILE] = rest

    def chunk(j):
        here = slice(j * TILE, (j + 1) * TILE)
        ids = lax.broadcasted_iota(jnp.int32, (TILE, TILE), 0)
        places = lax.broadcasted_iota(jnp.int32, (TILE, TILE), 1)
        corner = jnp.where(ids >= places, factor_ref[here, here], 0.0) + jnp.where(ids == places, 1.0, 0.0)
        factor = corner
        if j + 1 < count:
            factor = jnp.concatenate([corner, factor_ref[(j + 1) * TILE :, here]], axis=0)
        scaled = product((p_high[:, j * TILE :], p_low[:, j * TILE :]), halves(factor), ((1,), (0,)))
        band[j, span(col * piece_rows, piece_rows)] = scaled
        l_high[:, here], l_low[:, here] = halves(jnp.concatenate([scaled, f_ref[:, here]], axis=0))

        def piece_of(at, k):
            return band.at[j, span((2 * at + k) * piece_rows, piece_rows)]

        def hop(way, s):
            begun = line - way * (s - 1)
            came = line - way * s
            n = 0 if way > 0 else 1
            go = (line + way >= 0) & (line + way < line_n) & (begun >= 0) & (begun < line_n)
            arrives = (came >= 0) & (came < line_n)
            sem = (j, n, s)
            return go, arrives, begun, came, sem

        def hop_copy(at, sem, way):
            place = piece_of(at, core)
            return remote(place, place, chain_send.at[sem], chain_recv.at[sem], (row, 2 * (line + way) + core))

        def swap(at, slot):
            place = piece_of(at, core)
            return remote(place, place, swap_send.at[j, slot], swap_recv.at[j, slot], other_core)

        for s in range(1, line_n):
            for way in (1, -1):
                go, _, begun, _, sem = hop(way, s)

                @pl.when(go)
                def _():
                    hop_copy(begun, sem, way).start()

            if s == 1:
                swap(line, 0).start()
            yield
            for way in (1, -1):
                _, arrives, _, came, sem = hop(way, s)
                slot = 2 * s - 1 if way > 0 else 2 * s

                @pl.when(arrives)
                def _():
                    hop_copy(came, sem, way).wait_recv()
                    swap(came, slot).start()

        for s in range(1, line_n):
            for way in (1, -1):
                go, arrives, begun, came, sem = hop(way, s)
                slot = 2 * s - 1 if way > 0 else 2 * s

                @pl.when(go)
                def _():
                    hop_copy(begun, sem, way).wait_send()

                @pl.when(arrives)
                def _():
                    swap(came, slot).wait()

        swap(line, 0).wait()
        partial[j] = product((at_high[...], at_low[...]), halves(band[j]), ((1,), (0,)))
        copies = []
        for d in range(1, rows_n):
            to = (row + d) % rows_n
            src = partial.at[j, span(to * piece_rows, piece_rows)]
            copies.append(begin(src, got_part.at[j, d], part_send.at[j, d], part_recv.at[j, d], row_peers[d - 1]))
        yield
        for copy in copies:
            copy.wait()
        value = partial[j, span(row * piece_rows, piece_rows)]
        for d in range(1, rows_n):
            value = value + got_part[j, d]
        raw[j] = value
        move = lambda: remote(raw.at[j], moved.at[j], move_send.at[j], move_recv.at[j], target)

        @pl.when(jnp.logical_not(stays))
        def _():
            move().start()

        @pl.when(stays)
        def _():
            moved[j] = raw[j]

        yield

        @pl.when(jnp.logical_not(stays))
        def _():
            move().wait()

        full = (count - j) * TILE
        total = chunk_rows[j]
        base = sum(chunk_rows[:j])
        right = halves(jnp.concatenate([moved[j], f_ref[:, here]], axis=0))
        tiles[base : base + full] = product((l_high[:, j * TILE :], l_low[:, j * TILE :]), right, ((0,), (0,)))
        if total > full:
            tiles[base + full : base + total] = jnp.zeros((total - full, TILE), jnp.float32)
        half, part = total // 2, total // (2 * rows_n)
        piece = part // line_n
        base_half, base_part, base_piece = base // 2, base // (2 * rows_n), base // (2 * rows_n * line_n)
        src = tiles.at[span(base + (1 - core) * half, half)]
        copy = begin(src, got_core.at[base_half : base_half + half], sum_send.at[j, 0], core_recv.at[j], other_core)
        yield
        copy.wait()
        own = span(base + core * half, half)
        sums[base_half : base_half + half] = tiles[own] + got_core[base_half : base_half + half]
        here_part = slice(base_part, base_part + part)
        copies = []
        for d in range(1, rows_n):
            to = (row + d) % rows_n
            src = sums.at[span(base_half + to * part, part)]
            copies.append(
                begin(src, got_row.at[d, here_part], sum_send.at[j, d], row_recv.at[j, d], row_peers[d - 1])
            )
        yield
        for copy in copies:
            copy.wait()
        value = sums[span(base_half + row * part, part)]
        for d in range(1, rows_n):
            value = value + got_row[d, here_part]
        got_row[0, here_part] = value
        here_piece = slice(base_piece, base_piece + piece)
        copies = []
        for d in range(1, line_n):
            to = (line + d) % line_n
            src = got_row.at[0, span(base_part + to * piece, piece)]
            copies.append(
                begin(src, got_line.at[d, here_piece], sum_send.at[j, d], line_recv.at[j, d], line_peers[d - 1])
            )
        yield
        for copy in copies:
            copy.wait()
        value = got_row[0, span(base_part + line * piece, piece)]
        for d in range(1, line_n):
            value = value + got_line[d, here_piece]
        mine = span(base + core * half + row * part + line * piece, piece)
        whole[mine] = value
        copies = [
            begin(whole.at[mine], whole.at[mine], sum_send.at[j, d], back_line.at[j, d], line_peers[d - 1])
            for d in range(1, line_n)
        ]
        yield
        for copy in copies:
            copy.wait()
        mine = span(base + core * half + row * part, part)
        copies = [
            begin(whole.at[mine], whole.at[mine], sum_send.at[j, d], back_row.at[j, d], row_peers[d - 1])
            for d in range(1, rows_n)
        ]
        yield
        for copy in copies:
            copy.wait()
        mine = span(base + core * half, half)
        copy = begin(whole.at[mine], whole.at[mine], sum_send.at[j, 0], back_core.at[j], other_core)
        yield
        copy.wait()

    waiting = [chunk(j) for j in range(count)]
    active = []
    first = True
    while waiting or active:
        if waiting:
            active.append(waiting.pop(0))
        active = [flow for flow in active if next(flow, "end") != "end"]
        if first:
            prepare()
            first = False


def write_out(chunk_rows, moved, whole, sigma_ref, diag_ref):
    count = moved.shape[0]
    step_rows = sigma_ref.shape[0]
    step = pl.program_id(0)
    for i in range(count):

        @pl.when(step == i)
        def _():
            for j in range(count):
                low, high = min(i, j), max(i, j)
                at = sum(chunk_rows[:low]) + (high - low) * TILE
                tile = whole[at : at + TILE]
                diag_ref[:, j * TILE : (j + 1) * TILE] = tile if i >= j else tile.T
                sigma_ref[:, j * TILE : (j + 1) * TILE] = -moved[j, i * step_rows : (i + 1) * step_rows]


def finish(pattern, panel_pattern, inverse, panel, factor):
    rows_n = lax.axis_size("row")
    cols_n = lax.axis_size("col")
    line_n = cols_n // 2
    piece_rows, width = panel.shape
    block_rows, block_cols = inverse.shape
    count = width // TILE
    shares = 2 * rows_n * line_n
    chunk_rows = tuple(-(-(count - j) * TILE // (8 * shares)) * 8 * shares for j in range(count))
    total = sum(chunk_rows)
    most = max(rows_n, line_n)
    dma = pltpu.SemaphoreType.DMA
    vmem = pl.BlockSpec(memory_space=pltpu.VMEM)
    smem = pl.BlockSpec(memory_space=pltpu.SMEM)
    f32, b16 = jnp.float32, jnp.bfloat16
    moved, whole = pl.pallas_call(
        functools.partial(body, chunk_rows),
        out_shape=(
            jax.ShapeDtypeStruct((count, piece_rows, TILE), f32),
            jax.ShapeDtypeStruct((total, TILE), f32),
        ),
        in_specs=[smem, smem, vmem, vmem, vmem],
        out_specs=(vmem, vmem),
        scratch_shapes=[
            pltpu.VMEM((block_cols, block_rows), b16),
            pltpu.VMEM((block_cols, block_rows), b16),
            pltpu.VMEM((piece_rows, width), b16),
            pltpu.VMEM((piece_rows, width), b16),
            pltpu.VMEM((piece_rows + SHARE, width), b16),
            pltpu.VMEM((piece_rows + SHARE, width), b16),
            pltpu.VMEM((SHARE, width), f32),
            pltpu.VMEM((count, block_rows, TILE), f32),
            pltpu.VMEM((count, block_cols, TILE), f32),
            pltpu.VMEM((count, rows_n, piece_rows, TILE), f32),
            pltpu.VMEM((count, piece_rows, TILE), f32),
            pltpu.VMEM((total, TILE), f32),
            pltpu.VMEM((total // 2, TILE), f32),
            pltpu.VMEM((total // 2, TILE), f32),
            pltpu.VMEM((rows_n, total // (2 * rows_n), TILE), f32),
            pltpu.VMEM((line_n, total // shares, TILE), f32),
            dma((count, 2, line_n)),
            dma((count, 2, line_n)),
            dma((count, 2 * line_n)),
            dma((count, 2 * line_n)),
            dma((count, rows_n)),
            dma((count, rows_n)),
            dma((count,)),
            dma((count,)),
            dma((count, most)),
            dma((count,)),
            dma((count, rows_n)),
            dma((count, line_n)),
            dma((count, line_n)),
            dma((count, rows_n)),
            dma((count,)),
        ],
        compiler_params=pltpu.CompilerParams(collective_id=0, has_side_effects=True, vmem_limit_bytes=56 << 20),
    )(pattern, panel_pattern, inverse, panel, factor)
    return pl.pallas_call(
        functools.partial(write_out, chunk_rows),
        grid=(count,),
        out_shape=(jax.ShapeDtypeStruct((piece_rows, width), f32), jax.ShapeDtypeStruct((width, width), f32)),
        in_specs=[
            pl.BlockSpec((count, piece_rows, TILE), lambda i: (0, 0, 0)),
            pl.BlockSpec((total, TILE), lambda i: (0, 0)),
        ],
        out_specs=(
            pl.BlockSpec((piece_rows // count, width), lambda i: (i, 0)),
            pl.BlockSpec((TILE, width), lambda i: (i, 0)),
        ),
        compiler_params=pltpu.CompilerParams(vmem_limit_bytes=32 << 20),
    )(moved, whole)


def shards(ancestor_inverse, panel, diag_inverse, inverse_pattern, panel_pattern):
    return finish(inverse_pattern, panel_pattern, ancestor_inverse, panel, diag_inverse)


def solution(mesh):
    return jax.shard_map(
        shards,
        mesh=mesh,
        in_specs=(P("row", "col"), P(("row", "col"), None), P(), P(), P()),
        out_specs=(P(("row", "col"), None), P()),
        check_vma=False,
    )
```

```python
import functools

import jax
import jax.numpy as jnp
from jax import lax
from jax.experimental import pallas as pl
from jax.experimental.pallas import tpu as pltpu
from jax.sharding import PartitionSpec as P

TILE = 256
SHARE = 32


MESH = pl.DeviceIdType.MESH


def halves(value):
    top = value.astype(jnp.bfloat16)
    return top, (value - top.astype(jnp.float32)).astype(jnp.bfloat16)


def product(left, right, dims):
    dot = lambda a, b: lax.dot_general(a, b, (dims, ((), ())), preferred_element_type=jnp.float32)
    return dot(left[0], right[0]) + (dot(left[0], right[1]) + dot(left[1], right[0]))


def body(
    chunk_rows, flags_ref, panel_flags_ref, inv_ref, panel_ref, factor_ref, moved, whole,
    at_high, at_low, p_high, p_low, l_high, l_low, f_ref, band, partial, got_part, raw,
    tiles, got_core, sums, got_row, got_line,
    chain_send, chain_recv, swap_send, swap_recv, part_send, part_recv, move_send, move_recv,
    sum_send, core_recv, row_recv, line_recv, back_line, back_row, back_core,
):
    rows_n, cols_n = lax.axis_size("row"), lax.axis_size("col")
    line_n = cols_n // 2
    row, col = lax.axis_index("row"), lax.axis_index("col")
    line, core = col // 2, col % 2
    block_rows, block_cols = inv_ref.shape
    piece_rows, width = panel_ref.shape
    count = width // TILE
    other_core = (row, 2 * line + 1 - core)
    row_peers = [((row + d) % rows_n, col) for d in range(1, rows_n)]
    line_peers = [(row, 2 * ((line + d) % line_n) + core) for d in range(1, line_n)]
    peers = [other_core] + row_peers + line_peers
    target_at = col * rows_n + row
    target = (target_at // cols_n, target_at % cols_n)
    own_at = row * cols_n + col
    source = (own_at % rows_n, own_at // rows_n)
    stays = target_at == own_at

    barrier = pltpu.get_barrier_semaphore()
    for peer in peers:
        pl.semaphore_signal(barrier, inc=1, device_id=peer, device_id_type=MESH)

    @pl.when(jnp.logical_not(stays))
    def _():
        pl.semaphore_signal(barrier, inc=1, device_id=source, device_id_type=MESH)

    share = width // (rows_n * cols_n)
    first = own_at * share
    start = first // SHARE * SHARE
    ids = start + lax.broadcasted_iota(jnp.int32, (SHARE, width), 0)
    places = lax.broadcasted_iota(jnp.int32, (SHARE, width), 1)
    rows = jnp.where(ids >= places, factor_ref[pl.ds(pl.multiple_of(start, 8), SHARE)], 0.0)
    rows = rows + jnp.where(ids == places, 1.0, 0.0)
    f_ref[...] = jnp.where((ids >= first) & (ids < first + share), rows, 0.0)
    for k in range(count):
        here = slice(k * TILE, (k + 1) * TILE)
        flag = panel_flags_ref[own_at * piece_rows // TILE, k].astype(jnp.float32)
        p_high[:, here], p_low[:, here] = halves(panel_ref[:, here] * flag)

    @pl.when(stays)
    def _():
        pl.semaphore_wait(barrier, len(peers))

    @pl.when(jnp.logical_not(stays))
    def _():
        pl.semaphore_wait(barrier, len(peers) + 1)

    def span(start, size):
        return pl.ds(pl.multiple_of(start, 8), size)

    def remote(src, dst, send_sem, recv_sem, peer):
        return pltpu.make_async_remote_copy(
            src_ref=src, dst_ref=dst, send_sem=send_sem, recv_sem=recv_sem, device_id=peer, device_id_type=MESH
        )

    def begin(src, dst, send_sem, recv_sem, peer):
        copy = remote(src, dst, send_sem, recv_sem, peer)
        copy.start()
        return copy

    def prepare():
        for a in range(block_rows // TILE):
            for b in range(block_cols // TILE):
                flag = flags_ref[row * (block_rows // TILE) + a, col * (block_cols // TILE) + b].astype(jnp.float32)
                tile = inv_ref[a * TILE : (a + 1) * TILE, b * TILE : (b + 1) * TILE] * flag
                top, rest = halves(tile.T)
                at_high[b * TILE : (b + 1) * TILE, a * TILE : (a + 1) * TILE] = top
                at_low[b * TILE : (b + 1) * TILE, a * TILE : (a + 1) * TILE] = rest

    def chunk(j):
        here = slice(j * TILE, (j + 1) * TILE)
        ids = lax.broadcasted_iota(jnp.int32, (TILE, TILE), 0)
        places = lax.broadcasted_iota(jnp.int32, (TILE, TILE), 1)
        corner = jnp.where(ids >= places, factor_ref[here, here], 0.0) + jnp.where(ids == places, 1.0, 0.0)
        factor = corner
        if j + 1 < count:
            factor = jnp.concatenate([corner, factor_ref[(j + 1) * TILE :, here]], axis=0)
        scaled = product((p_high[:, j * TILE :], p_low[:, j * TILE :]), halves(factor), ((1,), (0,)))
        band[j, span(col * piece_rows, piece_rows)] = scaled
        l_high[:, here], l_low[:, here] = halves(jnp.concatenate([scaled, f_ref[:, here]], axis=0))

        def piece_of(at, k):
            return band.at[j, span((2 * at + k) * piece_rows, piece_rows)]

        def hop(way, s):
            begun = line - way * (s - 1)
            came = line - way * s
            n = 0 if way > 0 else 1
            go = (line + way >= 0) & (line + way < line_n) & (begun >= 0) & (begun < line_n)
            arrives = (came >= 0) & (came < line_n)
            sem = (j, n, s)
            return go, arrives, begun, came, sem

        def hop_copy(at, sem, way):
            place = piece_of(at, core)
            return remote(place, place, chain_send.at[sem], chain_recv.at[sem], (row, 2 * (line + way) + core))

        def swap(at, slot):
            place = piece_of(at, core)
            return remote(place, place, swap_send.at[j, slot], swap_recv.at[j, slot], other_core)

        for s in range(1, line_n):
            for way in (1, -1):
                go, _, begun, _, sem = hop(way, s)

                @pl.when(go)
                def _():
                    hop_copy(begun, sem, way).start()

            if s == 1:
                swap(line, 0).start()
            yield "line", 2 * piece_rows, 0.5
            for way in (1, -1):
                _, arrives, _, came, sem = hop(way, s)
                slot = 2 * s - 1 if way > 0 else 2 * s

                @pl.when(arrives)
                def _():
                    hop_copy(came, sem, way).wait_recv()
                    swap(came, slot).start()

        for s in range(1, line_n):
            for way in (1, -1):
                go, arrives, begun, came, sem = hop(way, s)
                slot = 2 * s - 1 if way > 0 else 2 * s

                @pl.when(go)
                def _():
                    hop_copy(begun, sem, way).wait_send()

                @pl.when(arrives)
                def _():
                    swap(came, slot).wait()

        swap(line, 0).wait()
        partial[j] = product((at_high[...], at_low[...]), halves(band[j]), ((1,), (0,)))
        copies = []
        for d in range(1, rows_n):
            to = (row + d) % rows_n
            src = partial.at[j, span(to * piece_rows, piece_rows)]
            copies.append(begin(src, got_part.at[j, d], part_send.at[j, d], part_recv.at[j, d], row_peers[d - 1]))
        yield "plane", 4 * piece_rows * (rows_n - 1) / 3, 3.0
        for copy in copies:
            copy.wait()
        value = partial[j, span(row * piece_rows, piece_rows)]
        for d in range(1, rows_n):
            value = value + got_part[j, d]
        raw[j] = value
        move = lambda: remote(raw.at[j], moved.at[j], move_send.at[j], move_recv.at[j], target)

        @pl.when(jnp.logical_not(stays))
        def _():
            move().start()

        @pl.when(stays)
        def _():
            moved[j] = raw[j]

        yield "plane", 2 * piece_rows, 0.5

        @pl.when(jnp.logical_not(stays))
        def _():
            move().wait()

        full = (count - j) * TILE
        total = chunk_rows[j]
        base = sum(chunk_rows[:j])
        right = halves(jnp.concatenate([moved[j], f_ref[:, here]], axis=0))
        tiles[base : base + full] = product((l_high[:, j * TILE :], l_low[:, j * TILE :]), right, ((0,), (0,)))
        if total > full:
            tiles[base + full : base + total] = jnp.zeros((total - full, TILE), jnp.float32)
        half, part = total // 2, total // (2 * rows_n)
        piece = part // line_n
        base_half, base_part, base_piece = base // 2, base // (2 * rows_n), base // (2 * rows_n * line_n)
        src = tiles.at[span(base + (1 - core) * half, half)]
        copy = begin(src, got_core.at[base_half : base_half + half], sum_send.at[j, 0], core_recv.at[j], other_core)
        yield "core", half, 1.0
        copy.wait()
        own = span(base + core * half, half)
        sums[base_half : base_half + half] = tiles[own] + got_core[base_half : base_half + half]
        here_part = slice(base_part, base_part + part)
        copies = []
        for d in range(1, rows_n):
            to = (row + d) % rows_n
            src = sums.at[span(base_half + to * part, part)]
            copies.append(
                begin(src, got_row.at[d, here_part], sum_send.at[j, d], row_recv.at[j, d], row_peers[d - 1])
            )
        yield "plane", 4 * part, 0.5
        for copy in copies:
            copy.wait()
        value = sums[span(base_half + row * part, part)]
        for d in range(1, rows_n):
            value = value + got_row[d, here_part]
        got_row[0, here_part] = value
        here_piece = slice(base_piece, base_piece + piece)
        copies = []
        for d in range(1, line_n):
            to = (line + d) % line_n
            src = got_row.at[0, span(base_part + to * piece, piece)]
            copies.append(
                begin(src, got_line.at[d, here_piece], sum_send.at[j, d], line_recv.at[j, d], line_peers[d - 1])
            )
        yield "line", 8 * piece, 0.5
        for copy in copies:
            copy.wait()
        value = got_row[0, span(base_part + line * piece, piece)]
        for d in range(1, line_n):
            value = value + got_line[d, here_piece]
        mine = span(base + core * half + row * part + line * piece, piece)
        whole[mine] = value
        copies = [
            begin(whole.at[mine], whole.at[mine], sum_send.at[j, d], back_line.at[j, d], line_peers[d - 1])
            for d in range(1, line_n)
        ]
        yield "line", 8 * piece, 0.5
        for copy in copies:
            copy.wait()
        mine = span(base + core * half + row * part, part)
        copies = [
            begin(whole.at[mine], whole.at[mine], sum_send.at[j, d], back_row.at[j, d], row_peers[d - 1])
            for d in range(1, rows_n)
        ]
        yield "plane", 4 * part, 0.5
        for copy in copies:
            copy.wait()
        mine = span(base + core * half, half)
        copy = begin(whole.at[mine], whole.at[mine], sum_send.at[j, 0], back_core.at[j], other_core)
        yield "core", half, 0.5
        copy.wait()

    free = {"line": 0.0, "plane": 0.0, "core": 0.0}
    now = 0.0
    events = [(4.0 * j, j, chunk(j)) for j in range(count)]
    first = True
    while events:
        events.sort(key=lambda event: event[:2])
        due, j, flow = events.pop(0)
        now = max(now, due)
        step = next(flow, None)
        if step is not None:
            link, kilobytes, work = step
            now += work
            rate = 300.0 if link == "core" else 85.0
            free[link] = max(free[link], now) + kilobytes / rate
            events.append((free[link] + 1.5, j, flow))
        if first:
            prepare()
            now += 3.0
            first = False


def write_out(chunk_rows, moved, whole, sigma_ref, diag_ref):
    count = moved.shape[0]
    step_rows = sigma_ref.shape[0]
    step = pl.program_id(0)
    for i in range(count):

        @pl.when(step == i)
        def _():
            for j in range(count):
                low, high = min(i, j), max(i, j)
                at = sum(chunk_rows[:low]) + (high - low) * TILE
                tile = whole[at : at + TILE]
                diag_ref[:, j * TILE : (j + 1) * TILE] = tile if i >= j else tile.T
                sigma_ref[:, j * TILE : (j + 1) * TILE] = -moved[j, i * step_rows : (i + 1) * step_rows]


def finish(pattern, panel_pattern, inverse, panel, factor):
    rows_n = lax.axis_size("row")
    cols_n = lax.axis_size("col")
    line_n = cols_n // 2
    piece_rows, width = panel.shape
    block_rows, block_cols = inverse.shape
    count = width // TILE
    shares = 2 * rows_n * line_n
    chunk_rows = tuple(-(-(count - j) * TILE // (8 * shares)) * 8 * shares for j in range(count))
    total = sum(chunk_rows)
    most = max(rows_n, line_n)
    dma = pltpu.SemaphoreType.DMA
    vmem = pl.BlockSpec(memory_space=pltpu.VMEM)
    smem = pl.BlockSpec(memory_space=pltpu.SMEM)
    f32, b16 = jnp.float32, jnp.bfloat16
    moved, whole = pl.pallas_call(
        functools.partial(body, chunk_rows),
        out_shape=(
            jax.ShapeDtypeStruct((count, piece_rows, TILE), f32),
            jax.ShapeDtypeStruct((total, TILE), f32),
        ),
        in_specs=[smem, smem, vmem, vmem, vmem],
        out_specs=(vmem, vmem),
        scratch_shapes=[
            pltpu.VMEM((block_cols, block_rows), b16),
            pltpu.VMEM((block_cols, block_rows), b16),
            pltpu.VMEM((piece_rows, width), b16),
            pltpu.VMEM((piece_rows, width), b16),
            pltpu.VMEM((piece_rows + SHARE, width), b16),
            pltpu.VMEM((piece_rows + SHARE, width), b16),
            pltpu.VMEM((SHARE, width), f32),
            pltpu.VMEM((count, block_rows, TILE), f32),
            pltpu.VMEM((count, block_cols, TILE), f32),
            pltpu.VMEM((count, rows_n, piece_rows, TILE), f32),
            pltpu.VMEM((count, piece_rows, TILE), f32),
            pltpu.VMEM((total, TILE), f32),
            pltpu.VMEM((total // 2, TILE), f32),
            pltpu.VMEM((total // 2, TILE), f32),
            pltpu.VMEM((rows_n, total // (2 * rows_n), TILE), f32),
            pltpu.VMEM((line_n, total // shares, TILE), f32),
            dma((count, 2, line_n)),
            dma((count, 2, line_n)),
            dma((count, 2 * line_n)),
            dma((count, 2 * line_n)),
            dma((count, rows_n)),
            dma((count, rows_n)),
            dma((count,)),
            dma((count,)),
            dma((count, most)),
            dma((count,)),
            dma((count, rows_n)),
            dma((count, line_n)),
            dma((count, line_n)),
            dma((count, rows_n)),
            dma((count,)),
        ],
        compiler_params=pltpu.CompilerParams(collective_id=0, has_side_effects=True, vmem_limit_bytes=56 << 20),
    )(pattern, panel_pattern, inverse, panel, factor)
    return pl.pallas_call(
        functools.partial(write_out, chunk_rows),
        grid=(count,),
        out_shape=(jax.ShapeDtypeStruct((piece_rows, width), f32), jax.ShapeDtypeStruct((width, width), f32)),
        in_specs=[
            pl.BlockSpec((count, piece_rows, TILE), lambda i: (0, 0, 0)),
            pl.BlockSpec((total, TILE), lambda i: (0, 0)),
        ],
        out_specs=(
            pl.BlockSpec((piece_rows // count, width), lambda i: (i, 0)),
            pl.BlockSpec((TILE, width), lambda i: (i, 0)),
        ),
        compiler_params=pltpu.CompilerParams(vmem_limit_bytes=32 << 20),
    )(moved, whole)


def shards(ancestor_inverse, panel, diag_inverse, inverse_pattern, panel_pattern):
    return finish(inverse_pattern, panel_pattern, ancestor_inverse, panel, diag_inverse)


def solution(mesh):
    return jax.shard_map(
        shards,
        mesh=mesh,
        in_specs=(P("row", "col"), P(("row", "col"), None), P(), P(), P()),
        out_specs=(P(("row", "col"), None), P()),
        check_vma=False,
    )
```

```python
import functools
import math

import jax
import jax.numpy as jnp
from jax import lax
from jax.experimental import pallas as pl
from jax.experimental.pallas import tpu as pltpu
from jax.sharding import PartitionSpec as P

TILE = 256
SHARE = 32


MESH = pl.DeviceIdType.MESH


def plane_of(rows_n):
    side = math.isqrt(rows_n)
    return (side, side) if side * side == rows_n else (rows_n, 1)


def halves(value):
    top = value.astype(jnp.bfloat16)
    return top, (value - top.astype(jnp.float32)).astype(jnp.bfloat16)


def product(left, right, dims):
    dot = lambda a, b: lax.dot_general(a, b, (dims, ((), ())), preferred_element_type=jnp.float32)
    return dot(left[0], right[0]) + (dot(left[0], right[1]) + dot(left[1], right[0]))


def body(
    chunk_rows, flags_ref, panel_flags_ref, inv_ref, panel_ref, factor_ref, moved, whole,
    at_high, at_low, p_high, p_low, l_high, l_low, f_ref, band, partial, part_one, part_mid, part_two, raw,
    tiles, got_core, sum_one, sum_mid, sum_two, got_row, got_line,
    chain_send, chain_recv, swap_send, swap_recv, part_send, part_recv, move_send, move_recv,
    row_send, row_recv, gather_send, gather_recv, sum_send, core_recv, line_recv, back_line, back_core,
):
    rows_n, cols_n = lax.axis_size("row"), lax.axis_size("col")
    line_n = cols_n // 2
    row, col = lax.axis_index("row"), lax.axis_index("col")
    line, core = col // 2, col % 2
    block_rows, block_cols = inv_ref.shape
    piece_rows, width = panel_ref.shape
    count = width // TILE
    other_core = (row, 2 * line + 1 - core)
    wide, tall = plane_of(rows_n)
    px, py = row % wide, row // wide
    x_at = [(px + d) % wide for d in range(wide)]
    y_at = [(py + d) % tall for d in range(tall)]
    x_peers = [(py * wide + x_at[d], col) for d in range(wide)]
    y_peers = [(y_at[d] * wide + px, col) for d in range(tall)]
    line_peers = [(row, 2 * ((line + d) % line_n) + core) for d in range(1, line_n)]
    peers = [other_core] + x_peers[1:] + y_peers[1:] + line_peers
    target_at = col * rows_n + row
    target = (target_at // cols_n, target_at % cols_n)
    own_at = row * cols_n + col
    source = (own_at % rows_n, own_at // rows_n)
    stays = target_at == own_at

    barrier = pltpu.get_barrier_semaphore()
    for peer in peers:
        pl.semaphore_signal(barrier, inc=1, device_id=peer, device_id_type=MESH)

    @pl.when(jnp.logical_not(stays))
    def _():
        pl.semaphore_signal(barrier, inc=1, device_id=source, device_id_type=MESH)

    share = width // (rows_n * cols_n)
    first = own_at * share
    start = first // SHARE * SHARE
    ids = start + lax.broadcasted_iota(jnp.int32, (SHARE, width), 0)
    places = lax.broadcasted_iota(jnp.int32, (SHARE, width), 1)
    rows = jnp.where(ids >= places, factor_ref[pl.ds(pl.multiple_of(start, 8), SHARE)], 0.0)
    rows = rows + jnp.where(ids == places, 1.0, 0.0)
    f_ref[...] = jnp.where((ids >= first) & (ids < first + share), rows, 0.0)
    for k in range(count):
        here = slice(k * TILE, (k + 1) * TILE)
        flag = panel_flags_ref[own_at * piece_rows // TILE, k].astype(jnp.float32)
        p_high[:, here], p_low[:, here] = halves(panel_ref[:, here] * flag)

    @pl.when(stays)
    def _():
        pl.semaphore_wait(barrier, len(peers))

    @pl.when(jnp.logical_not(stays))
    def _():
        pl.semaphore_wait(barrier, len(peers) + 1)

    def span(start, size):
        return pl.ds(pl.multiple_of(start, 8), size)

    def remote(src, dst, send_sem, recv_sem, peer):
        return pltpu.make_async_remote_copy(
            src_ref=src, dst_ref=dst, send_sem=send_sem, recv_sem=recv_sem, device_id=peer, device_id_type=MESH
        )

    def begin(src, dst, send_sem, recv_sem, peer):
        copy = remote(src, dst, send_sem, recv_sem, peer)
        copy.start()
        return copy

    left, right_half = slice(0, TILE // 2), slice(TILE // 2, TILE)

    def plane_sum(j, view, rows, got_one, middle, got_two, send, recv, n):
        copies = []
        for d in range(1, wide):
            for y in range(tall):
                slot = d * tall + y
                src = view(y * wide + x_at[d]).at[:, left]
                copies.append(begin(src, got_one.at[0, slot, rows], send.at[j, 0, slot], recv.at[j, 0, slot], x_peers[d]))
        for d in range(1, tall):
            for x in range(wide):
                slot = d * wide + x
                src = view(y_at[d] * wide + x).at[:, right_half]
                copies.append(begin(src, got_one.at[1, slot, rows], send.at[j, 1, slot], recv.at[j, 1, slot], y_peers[d]))
        yield "plane", 2 * n, 1.0
        for copy in copies:
            copy.wait()
        for y in range(tall):
            value = view(y * wide + px)[:, left]
            for d in range(1, wide):
                value = value + got_one[0, d * tall + y, rows]
            middle[0, y, rows] = value
        for x in range(wide):
            value = view(py * wide + x)[:, right_half]
            for d in range(1, tall):
                value = value + got_one[1, d * wide + x, rows]
            middle[1, x, rows] = value
        copies = []
        for d in range(1, tall):
            src = middle.at[0, y_at[d], rows]
            copies.append(begin(src, got_two.at[0, d, rows], send.at[j, 2, d], recv.at[j, 2, d], y_peers[d]))
        for d in range(1, wide):
            src = middle.at[1, x_at[d], rows]
            copies.append(begin(src, got_two.at[1, d, rows], send.at[j, 3, d], recv.at[j, 3, d], x_peers[d]))
        yield "plane", n, 0.5
        for copy in copies:
            copy.wait()
        one = middle[0, py, rows]
        for d in range(1, tall):
            one = one + got_two[0, d, rows]
        two = middle[1, px, rows]
        for d in range(1, wide):
            two = two + got_two[1, d, rows]
        return jnp.concatenate([one, two], axis=1)

    def plane_gather(j, view, send, recv, n):
        def share_out(place, half_cols, k, slot, peer):
            ref = view(place).at[:, half_cols]
            return begin(ref, ref, send.at[j, k, slot], recv.at[j, k, slot], peer)

        copies = [share_out(row, left, 0, d, x_peers[d]) for d in range(1, wide)]
        copies += [share_out(row, right_half, 1, d, y_peers[d]) for d in range(1, tall)]
        yield "plane", n, 0.5
        for copy in copies:
            copy.wait()
        copies = []
        for d in range(1, tall):
            for x in range(wide):
                copies.append(share_out(py * wide + x, left, 2, d * wide + x, y_peers[d]))
        for d in range(1, wide):
            for y in range(tall):
                copies.append(share_out(y * wide + px, right_half, 3, d * tall + y, x_peers[d]))
        yield "plane", 2 * n, 0.5
        for copy in copies:
            copy.wait()

    def prepare():
        for a in range(block_rows // TILE):
            for b in range(block_cols // TILE):
                flag = flags_ref[row * (block_rows // TILE) + a, col * (block_cols // TILE) + b].astype(jnp.float32)
                tile = inv_ref[a * TILE : (a + 1) * TILE, b * TILE : (b + 1) * TILE] * flag
                top, rest = halves(tile.T)
                at_high[b * TILE : (b + 1) * TILE, a * TILE : (a + 1) * TILE] = top
                at_low[b * TILE : (b + 1) * TILE, a * TILE : (a + 1) * TILE] = rest

    def chunk(j):
        here = slice(j * TILE, (j + 1) * TILE)
        ids = lax.broadcasted_iota(jnp.int32, (TILE, TILE), 0)
        places = lax.broadcasted_iota(jnp.int32, (TILE, TILE), 1)
        corner = jnp.where(ids >= places, factor_ref[here, here], 0.0) + jnp.where(ids == places, 1.0, 0.0)
        factor = corner
        if j + 1 < count:
            factor = jnp.concatenate([corner, factor_ref[(j + 1) * TILE :, here]], axis=0)
        scaled = product((p_high[:, j * TILE :], p_low[:, j * TILE :]), halves(factor), ((1,), (0,)))
        band[j, span(col * piece_rows, piece_rows)] = scaled
        l_high[:, here], l_low[:, here] = halves(jnp.concatenate([scaled, f_ref[:, here]], axis=0))

        def piece_of(at, k):
            return band.at[j, span((2 * at + k) * piece_rows, piece_rows)]

        def hop(way, s):
            begun = line - way * (s - 1)
            came = line - way * s
            n = 0 if way > 0 else 1
            go = (line + way >= 0) & (line + way < line_n) & (begun >= 0) & (begun < line_n)
            arrives = (came >= 0) & (came < line_n)
            sem = (j, n, s)
            return go, arrives, begun, came, sem

        def hop_copy(at, sem, way):
            place = piece_of(at, core)
            return remote(place, place, chain_send.at[sem], chain_recv.at[sem], (row, 2 * (line + way) + core))

        def swap(at, slot):
            place = piece_of(at, core)
            return remote(place, place, swap_send.at[j, slot], swap_recv.at[j, slot], other_core)

        for s in range(1, line_n):
            for way in (1, -1):
                go, _, begun, _, sem = hop(way, s)

                @pl.when(go)
                def _():
                    hop_copy(begun, sem, way).start()

            if s == 1:
                swap(line, 0).start()
            yield "line", 2 * piece_rows, 0.5
            for way in (1, -1):
                _, arrives, _, came, sem = hop(way, s)
                slot = 2 * s - 1 if way > 0 else 2 * s

                @pl.when(arrives)
                def _():
                    hop_copy(came, sem, way).wait_recv()
                    swap(came, slot).start()

        for s in range(1, line_n):
            for way in (1, -1):
                go, arrives, begun, came, sem = hop(way, s)
                slot = 2 * s - 1 if way > 0 else 2 * s

                @pl.when(go)
                def _():
                    hop_copy(begun, sem, way).wait_send()

                @pl.when(arrives)
                def _():
                    swap(came, slot).wait()

        swap(line, 0).wait()
        partial[j] = product((at_high[...], at_low[...]), halves(band[j]), ((1,), (0,)))
        raw[j] = yield from plane_sum(
            j,
            lambda i: partial.at[j, span(i * piece_rows, piece_rows)],
            slice(j * piece_rows, (j + 1) * piece_rows),
            part_one, part_mid, part_two, part_send, part_recv, piece_rows,
        )
        move = lambda: remote(raw.at[j], moved.at[j], move_send.at[j], move_recv.at[j], target)

        @pl.when(jnp.logical_not(stays))
        def _():
            move().start()

        @pl.when(stays)
        def _():
            moved[j] = raw[j]

        yield "plane", 2 * piece_rows, 0.5

        @pl.when(jnp.logical_not(stays))
        def _():
            move().wait()

        full = (count - j) * TILE
        total = chunk_rows[j]
        base = sum(chunk_rows[:j])
        right = halves(jnp.concatenate([moved[j], f_ref[:, here]], axis=0))
        tiles[base : base + full] = product((l_high[:, j * TILE :], l_low[:, j * TILE :]), right, ((0,), (0,)))
        if total > full:
            tiles[base + full : base + total] = jnp.zeros((total - full, TILE), jnp.float32)
        half, part = total // 2, total // (2 * rows_n)
        piece = part // line_n
        base_half, base_part, base_piece = base // 2, base // (2 * rows_n), base // (2 * rows_n * line_n)
        src = tiles.at[span(base + (1 - core) * half, half)]
        copy = begin(src, got_core.at[base_half : base_half + half], sum_send.at[j, 0], core_recv.at[j], other_core)
        yield "core", half, 1.0
        copy.wait()
        own = span(base + core * half, half)
        tiles[own] = tiles[own] + got_core[base_half : base_half + half]
        here_part = slice(base_part, base_part + part)
        got_row[here_part] = yield from plane_sum(
            j,
            lambda i: tiles.at[span(base + core * half + i * part, part)],
            here_part,
            sum_one, sum_mid, sum_two, row_send, row_recv, part,
        )
        here_piece = slice(base_piece, base_piece + piece)
        copies = []
        for d in range(1, line_n):
            to = (line + d) % line_n
            src = got_row.at[span(base_part + to * piece, piece)]
            copies.append(
                begin(src, got_line.at[d, here_piece], sum_send.at[j, d], line_recv.at[j, d], line_peers[d - 1])
            )
        yield "line", 8 * piece, 0.5
        for copy in copies:
            copy.wait()
        value = got_row[span(base_part + line * piece, piece)]
        for d in range(1, line_n):
            value = value + got_line[d, here_piece]
        mine = span(base + core * half + row * part + line * piece, piece)
        whole[mine] = value
        copies = [
            begin(whole.at[mine], whole.at[mine], sum_send.at[j, d], back_line.at[j, d], line_peers[d - 1])
            for d in range(1, line_n)
        ]
        yield "line", 8 * piece, 0.5
        for copy in copies:
            copy.wait()
        yield from plane_gather(
            j, lambda i: whole.at[span(base + core * half + i * part, part)], gather_send, gather_recv, part
        )
        mine = span(base + core * half, half)
        copy = begin(whole.at[mine], whole.at[mine], sum_send.at[j, 0], back_core.at[j], other_core)
        yield "core", half, 0.5
        copy.wait()

    free = {"line": 0.0, "plane": 0.0, "core": 0.0}
    now = 0.0
    events = [(4.0 * j, j, chunk(j)) for j in range(count)]
    first = True
    while events:
        events.sort(key=lambda event: event[:2])
        due, j, flow = events.pop(0)
        now = max(now, due)
        step = next(flow, None)
        if step is not None:
            link, kilobytes, work = step
            now += work
            rate = 300.0 if link == "core" else 85.0
            free[link] = max(free[link], now) + kilobytes / rate
            events.append((free[link] + 1.5, j, flow))
        if first:
            prepare()
            now += 3.0
            first = False


def write_out(chunk_rows, moved, whole, sigma_ref, diag_ref):
    count = moved.shape[0]
    step_rows = sigma_ref.shape[0]
    step = pl.program_id(0)
    for i in range(count):

        @pl.when(step == i)
        def _():
            for j in range(count):
                low, high = min(i, j), max(i, j)
                at = sum(chunk_rows[:low]) + (high - low) * TILE
                tile = whole[at : at + TILE]
                diag_ref[:, j * TILE : (j + 1) * TILE] = tile if i >= j else tile.T
                sigma_ref[:, j * TILE : (j + 1) * TILE] = -moved[j, i * step_rows : (i + 1) * step_rows]


def finish(pattern, panel_pattern, inverse, panel, factor):
    rows_n = lax.axis_size("row")
    cols_n = lax.axis_size("col")
    line_n = cols_n // 2
    piece_rows, width = panel.shape
    block_rows, block_cols = inverse.shape
    count = width // TILE
    shares = 2 * rows_n * line_n
    chunk_rows = tuple(-(-(count - j) * TILE // (8 * shares)) * 8 * shares for j in range(count))
    total = sum(chunk_rows)
    side = max(plane_of(rows_n))
    dma = pltpu.SemaphoreType.DMA
    vmem = pl.BlockSpec(memory_space=pltpu.VMEM)
    smem = pl.BlockSpec(memory_space=pltpu.SMEM)
    f32, b16 = jnp.float32, jnp.bfloat16
    moved, whole = pl.pallas_call(
        functools.partial(body, chunk_rows),
        out_shape=(
            jax.ShapeDtypeStruct((count, piece_rows, TILE), f32),
            jax.ShapeDtypeStruct((total, TILE), f32),
        ),
        in_specs=[smem, smem, vmem, vmem, vmem],
        out_specs=(vmem, vmem),
        scratch_shapes=[
            pltpu.VMEM((block_cols, block_rows), b16),
            pltpu.VMEM((block_cols, block_rows), b16),
            pltpu.VMEM((piece_rows, width), b16),
            pltpu.VMEM((piece_rows, width), b16),
            pltpu.VMEM((piece_rows + SHARE, width), b16),
            pltpu.VMEM((piece_rows + SHARE, width), b16),
            pltpu.VMEM((SHARE, width), f32),
            pltpu.VMEM((count, block_rows, TILE), f32),
            pltpu.VMEM((count, block_cols, TILE), f32),
            pltpu.VMEM((2, rows_n, count * piece_rows, TILE // 2), f32),
            pltpu.VMEM((2, side, count * piece_rows, TILE // 2), f32),
            pltpu.VMEM((2, side, count * piece_rows, TILE // 2), f32),
            pltpu.VMEM((count, piece_rows, TILE), f32),
            pltpu.VMEM((total, TILE), f32),
            pltpu.VMEM((total // 2, TILE), f32),
            pltpu.VMEM((2, rows_n, total // (2 * rows_n), TILE // 2), f32),
            pltpu.VMEM((2, side, total // (2 * rows_n), TILE // 2), f32),
            pltpu.VMEM((2, side, total // (2 * rows_n), TILE // 2), f32),
            pltpu.VMEM((total // (2 * rows_n), TILE), f32),
            pltpu.VMEM((line_n, total // shares, TILE), f32),
            dma((count, 2, line_n)),
            dma((count, 2, line_n)),
            dma((count, 2 * line_n)),
            dma((count, 2 * line_n)),
            dma((count, 4, rows_n)),
            dma((count, 4, rows_n)),
            dma((count,)),
            dma((count,)),
            dma((count, 4, rows_n)),
            dma((count, 4, rows_n)),
            dma((count, 4, rows_n)),
            dma((count, 4, rows_n)),
            dma((count, line_n)),
            dma((count,)),
            dma((count, line_n)),
            dma((count, line_n)),
            dma((count,)),
        ],
        compiler_params=pltpu.CompilerParams(collective_id=0, has_side_effects=True, vmem_limit_bytes=56 << 20),
    )(pattern, panel_pattern, inverse, panel, factor)
    return pl.pallas_call(
        functools.partial(write_out, chunk_rows),
        grid=(count,),
        out_shape=(jax.ShapeDtypeStruct((piece_rows, width), f32), jax.ShapeDtypeStruct((width, width), f32)),
        in_specs=[
            pl.BlockSpec((count, piece_rows, TILE), lambda i: (0, 0, 0)),
            pl.BlockSpec((total, TILE), lambda i: (0, 0)),
        ],
        out_specs=(
            pl.BlockSpec((piece_rows // count, width), lambda i: (i, 0)),
            pl.BlockSpec((TILE, width), lambda i: (i, 0)),
        ),
        compiler_params=pltpu.CompilerParams(vmem_limit_bytes=32 << 20),
    )(moved, whole)


def shards(ancestor_inverse, panel, diag_inverse, inverse_pattern, panel_pattern):
    return finish(inverse_pattern, panel_pattern, ancestor_inverse, panel, diag_inverse)


def solution(mesh):
    return jax.shard_map(
        shards,
        mesh=mesh,
        in_specs=(P("row", "col"), P(("row", "col"), None), P(), P(), P()),
        out_specs=(P(("row", "col"), None), P()),
        check_vma=False,
    )
```

```python
import functools

import jax
import jax.numpy as jnp
from jax import lax
from jax.experimental import pallas as pl
from jax.experimental.pallas import tpu as pltpu
from jax.sharding import PartitionSpec as P

TILE = 256
SHARE = 32


MESH = pl.DeviceIdType.MESH


def halves(value):
    top = value.astype(jnp.bfloat16)
    return top, (value - top.astype(jnp.float32)).astype(jnp.bfloat16)


def product(left, right, dims):
    dot = lambda a, b: lax.dot_general(a, b, (dims, ((), ())), preferred_element_type=jnp.float32)
    return dot(left[0], right[0]) + (dot(left[0], right[1]) + dot(left[1], right[0]))


def body(
    chunk_rows, flags_ref, panel_flags_ref, inv_ref, panel_ref, factor_ref, moved, whole,
    at_high, at_low, p_high, p_low, l_high, l_low, f_ref, band, x_there, partial, got_part, raw,
    tiles, got_core, got_row, got_line, got_full,
    chain_send, chain_recv, swap_send, swap_recv, part_send, part_recv, move_send, move_recv, ahead_send, ahead_recv,
    sum_send, core_recv, row_recv, line_recv, back_line, back_row, back_core,
):
    rows_n, cols_n = lax.axis_size("row"), lax.axis_size("col")
    line_n = cols_n // 2
    row, col = lax.axis_index("row"), lax.axis_index("col")
    line, core = col // 2, col % 2
    block_rows, block_cols = inv_ref.shape
    piece_rows, width = panel_ref.shape
    count = width // TILE
    other_core = (row, 2 * line + 1 - core)
    row_peers = [((row + d) % rows_n, col) for d in range(1, rows_n)]
    line_peers = [(row, 2 * ((line + d) % line_n) + core) for d in range(1, line_n)]
    peers = [other_core] + row_peers + line_peers
    target_at = col * rows_n + row
    target = (target_at // cols_n, target_at % cols_n)
    own_at = row * cols_n + col
    source = (own_at % rows_n, own_at // rows_n)
    stays = target_at == own_at

    barrier = pltpu.get_barrier_semaphore()
    for peer in peers:
        pl.semaphore_signal(barrier, inc=1, device_id=peer, device_id_type=MESH)

    @pl.when(jnp.logical_not(stays))
    def _():
        pl.semaphore_signal(barrier, inc=1, device_id=source, device_id_type=MESH)
        pl.semaphore_signal(barrier, inc=1, device_id=target, device_id_type=MESH)

    share = width // (rows_n * cols_n)
    first = own_at * share
    start = first // SHARE * SHARE
    ids = start + lax.broadcasted_iota(jnp.int32, (SHARE, width), 0)
    places = lax.broadcasted_iota(jnp.int32, (SHARE, width), 1)
    rows = jnp.where(ids >= places, factor_ref[pl.ds(pl.multiple_of(start, 8), SHARE)], 0.0)
    rows = rows + jnp.where(ids == places, 1.0, 0.0)
    f_ref[...] = jnp.where((ids >= first) & (ids < first + share), rows, 0.0)
    for k in range(count):
        here = slice(k * TILE, (k + 1) * TILE)
        flag = panel_flags_ref[own_at * piece_rows // TILE, k].astype(jnp.float32)
        p_high[:, here], p_low[:, here] = halves(panel_ref[:, here] * flag)

    @pl.when(stays)
    def _():
        pl.semaphore_wait(barrier, len(peers))

    @pl.when(jnp.logical_not(stays))
    def _():
        pl.semaphore_wait(barrier, len(peers) + 2)

    def span(start, size):
        return pl.ds(pl.multiple_of(start, 8), size)

    def remote(src, dst, send_sem, recv_sem, peer):
        return pltpu.make_async_remote_copy(
            src_ref=src, dst_ref=dst, send_sem=send_sem, recv_sem=recv_sem, device_id=peer, device_id_type=MESH
        )

    def begin(src, dst, send_sem, recv_sem, peer):
        copy = remote(src, dst, send_sem, recv_sem, peer)
        copy.start()
        return copy

    def prepare():
        for a in range(block_rows // TILE):
            for b in range(block_cols // TILE):
                flag = flags_ref[row * (block_rows // TILE) + a, col * (block_cols // TILE) + b].astype(jnp.float32)
                tile = inv_ref[a * TILE : (a + 1) * TILE, b * TILE : (b + 1) * TILE] * flag
                top, rest = halves(tile.T)
                at_high[b * TILE : (b + 1) * TILE, a * TILE : (a + 1) * TILE] = top
                at_low[b * TILE : (b + 1) * TILE, a * TILE : (a + 1) * TILE] = rest

    def ahead(j):
        mine = band.at[j, span(col * piece_rows, piece_rows)]
        return remote(mine, x_there.at[j], ahead_send.at[j], ahead_recv.at[j], source)

    def chunk(j):
        here = slice(j * TILE, (j + 1) * TILE)
        ids = lax.broadcasted_iota(jnp.int32, (TILE, TILE), 0)
        places = lax.broadcasted_iota(jnp.int32, (TILE, TILE), 1)
        corner = jnp.where(ids >= places, factor_ref[here, here], 0.0) + jnp.where(ids == places, 1.0, 0.0)
        factor = corner
        if j + 1 < count:
            factor = jnp.concatenate([corner, factor_ref[(j + 1) * TILE :, here]], axis=0)
        scaled = product((p_high[:, j * TILE :], p_low[:, j * TILE :]), halves(factor), ((1,), (0,)))
        band[j, span(col * piece_rows, piece_rows)] = scaled

        @pl.when(jnp.logical_not(stays))
        def _():
            ahead(j).start()

        @pl.when(stays)
        def _():
            x_there[j] = scaled


        def piece_of(at, k):
            return band.at[j, span((2 * at + k) * piece_rows, piece_rows)]

        def hop(way, s):
            begun = line - way * (s - 1)
            came = line - way * s
            n = 0 if way > 0 else 1
            go = (line + way >= 0) & (line + way < line_n) & (begun >= 0) & (begun < line_n)
            arrives = (came >= 0) & (came < line_n)
            sem = (j, n, s)
            return go, arrives, begun, came, sem

        def hop_copy(at, sem, way):
            place = piece_of(at, core)
            return remote(place, place, chain_send.at[sem], chain_recv.at[sem], (row, 2 * (line + way) + core))

        def swap(at, slot):
            place = piece_of(at, core)
            return remote(place, place, swap_send.at[j, slot], swap_recv.at[j, slot], other_core)

        for s in range(1, line_n):
            for way in (1, -1):
                go, _, begun, _, sem = hop(way, s)

                @pl.when(go)
                def _():
                    hop_copy(begun, sem, way).start()

            if s == 1:
                swap(line, 0).start()
            yield "line", 2 * piece_rows, 0.5
            for way in (1, -1):
                _, arrives, _, came, sem = hop(way, s)
                slot = 2 * s - 1 if way > 0 else 2 * s

                @pl.when(arrives)
                def _():
                    hop_copy(came, sem, way).wait_recv()
                    swap(came, slot).start()

        for s in range(1, line_n):
            for way in (1, -1):
                go, arrives, begun, came, sem = hop(way, s)
                slot = 2 * s - 1 if way > 0 else 2 * s

                @pl.when(go)
                def _():
                    hop_copy(begun, sem, way).wait_send()

                @pl.when(arrives)
                def _():
                    swap(came, slot).wait()

        swap(line, 0).wait()
        partial[j] = product((at_high[...], at_low[...]), halves(band[j]), ((1,), (0,)))
        copies = []
        for d in range(1, rows_n):
            to = (row + d) % rows_n
            src = partial.at[j, span(to * piece_rows, piece_rows)]
            copies.append(begin(src, got_part.at[j, d], part_send.at[j, d], part_recv.at[j, d], row_peers[d - 1]))
        yield "plane", 4 * piece_rows * (rows_n - 1) / 3, 3.0
        for copy in copies:
            copy.wait()
        value = partial[j, span(row * piece_rows, piece_rows)]
        for d in range(1, rows_n):
            value = value + got_part[j, d]
        raw[j] = value
        move = lambda: remote(raw.at[j], moved.at[j], move_send.at[j], move_recv.at[j], target)

        @pl.when(jnp.logical_not(stays))
        def _():
            move().start()

        @pl.when(stays)
        def _():
            moved[j] = raw[j]

        if j == 0:
            for k in range(count):

                @pl.when(jnp.logical_not(stays))
                def _():
                    ahead(k).wait()

                part_here = slice(k * TILE, (k + 1) * TILE)
                both = jnp.concatenate([x_there[k], f_ref[:, part_here]], axis=0)
                l_high[:, part_here], l_low[:, part_here] = halves(both)
        here = slice(j * TILE, (j + 1) * TILE)
        full = (count - j) * TILE
        total = chunk_rows[j]
        base = sum(chunk_rows[:j])
        right = halves(jnp.concatenate([raw[j], f_ref[:, here]], axis=0))
        tiles[base : base + full] = product((l_high[:, j * TILE :], l_low[:, j * TILE :]), right, ((0,), (0,)))
        if total > full:
            tiles[base + full : base + total] = jnp.zeros((total - full, TILE), jnp.float32)
        half, part = total // 2, total // (2 * rows_n)
        piece = part // line_n
        base_half, base_part, base_piece = base // 2, base // (2 * rows_n), base // (2 * rows_n * line_n)
        src = tiles.at[span(base + (1 - core) * half, half)]
        copy = begin(src, got_core.at[base_half : base_half + half], sum_send.at[j, 0], core_recv.at[j], other_core)
        yield "core", half, 1.0
        copy.wait()
        own = span(base + core * half, half)
        tiles[own] = tiles[own] + got_core[base_half : base_half + half]
        here_part = slice(base_part, base_part + part)
        copies = []
        for d in range(1, rows_n):
            to = (row + d) % rows_n
            src = tiles.at[span(base + core * half + to * part, part)]
            copies.append(
                begin(src, got_row.at[d, here_part], sum_send.at[j, d], row_recv.at[j, d], row_peers[d - 1])
            )
        yield "plane", 4 * part, 0.5
        for copy in copies:
            copy.wait()
        value = tiles[span(base + core * half + row * part, part)]
        for d in range(1, rows_n):
            value = value + got_row[d, here_part]
        got_row[0, here_part] = value
        if j == 0:
            here_piece = slice(base_piece, base_piece + piece)
            copies = []
            for d in range(1, line_n):
                to = (line + d) % line_n
                src = got_row.at[0, span(base_part + to * piece, piece)]
                copies.append(
                    begin(src, got_line.at[d, here_piece], sum_send.at[j, d], line_recv.at[j, d], line_peers[d - 1])
                )
            yield "line", 8 * piece, 0.5
            for copy in copies:
                copy.wait()
            value = got_row[0, span(base_part + line * piece, piece)]
            for d in range(1, line_n):
                value = value + got_line[d, here_piece]
            mine = span(base + core * half + row * part + line * piece, piece)
            whole[mine] = value
            copies = [
                begin(whole.at[mine], whole.at[mine], sum_send.at[j, d], back_line.at[j, d], line_peers[d - 1])
                for d in range(1, line_n)
            ]
            yield "line", 8 * piece, 0.5
            for copy in copies:
                copy.wait()
        else:
            copies = []
            for d in range(1, line_n):
                src = got_row.at[0, here_part]
                dst = got_full.at[line, here_part]
                copies.append(begin(src, dst, sum_send.at[j, d], line_recv.at[j, d], line_peers[d - 1]))
            got_full[line, here_part] = value
            yield "line", 8 * part, 0.5
            for copy in copies:
                copy.wait()
            value = got_full[0, here_part]
            for d in range(1, line_n):
                value = value + got_full[d, here_part]
            whole[span(base + core * half + row * part, part)] = value
        mine = span(base + core * half + row * part, part)
        copies = [
            begin(whole.at[mine], whole.at[mine], sum_send.at[j, d], back_row.at[j, d], row_peers[d - 1])
            for d in range(1, rows_n)
        ]
        yield "plane", 4 * part, 0.5
        for copy in copies:
            copy.wait()
        mine = span(base + core * half, half)
        copy = begin(whole.at[mine], whole.at[mine], sum_send.at[j, 0], back_core.at[j], other_core)
        yield "core", half, 0.5
        copy.wait()

        @pl.when(jnp.logical_not(stays))
        def _():
            move().wait()

    free = {"line": 0.0, "plane": 0.0, "core": 0.0}
    now = 0.0
    events = [(4.0 * j, j, chunk(j)) for j in range(count)]
    first = True
    while events:
        events.sort(key=lambda event: event[:2])
        due, j, flow = events.pop(0)
        now = max(now, due)
        step = next(flow, None)
        if step is not None:
            link, kilobytes, work = step
            now += work
            rate = 300.0 if link == "core" else 85.0
            free[link] = max(free[link], now) + kilobytes / rate
            events.append((free[link] + 1.5, j, flow))
        if first:
            prepare()
            now += 3.0
            first = False


def write_out(chunk_rows, moved, whole, sigma_ref, diag_ref):
    count = moved.shape[0]
    step_rows = sigma_ref.shape[0]
    step = pl.program_id(0)
    for i in range(count):

        @pl.when(step == i)
        def _():
            for j in range(count):
                low, high = min(i, j), max(i, j)
                at = sum(chunk_rows[:low]) + (high - low) * TILE
                tile = whole[at : at + TILE]
                diag_ref[:, j * TILE : (j + 1) * TILE] = tile if i >= j else tile.T
                sigma_ref[:, j * TILE : (j + 1) * TILE] = -moved[j, i * step_rows : (i + 1) * step_rows]


def finish(pattern, panel_pattern, inverse, panel, factor):
    rows_n = lax.axis_size("row")
    cols_n = lax.axis_size("col")
    line_n = cols_n // 2
    piece_rows, width = panel.shape
    block_rows, block_cols = inverse.shape
    count = width // TILE
    shares = 2 * rows_n * line_n
    chunk_rows = tuple(-(-(count - j) * TILE // (8 * shares)) * 8 * shares for j in range(count))
    total = sum(chunk_rows)
    most = max(rows_n, line_n)
    dma = pltpu.SemaphoreType.DMA
    vmem = pl.BlockSpec(memory_space=pltpu.VMEM)
    smem = pl.BlockSpec(memory_space=pltpu.SMEM)
    f32, b16 = jnp.float32, jnp.bfloat16
    moved, whole = pl.pallas_call(
        functools.partial(body, chunk_rows),
        out_shape=(
            jax.ShapeDtypeStruct((count, piece_rows, TILE), f32),
            jax.ShapeDtypeStruct((total, TILE), f32),
        ),
        in_specs=[smem, smem, vmem, vmem, vmem],
        out_specs=(vmem, vmem),
        scratch_shapes=[
            pltpu.VMEM((block_cols, block_rows), b16),
            pltpu.VMEM((block_cols, block_rows), b16),
            pltpu.VMEM((piece_rows, width), b16),
            pltpu.VMEM((piece_rows, width), b16),
            pltpu.VMEM((piece_rows + SHARE, width), b16),
            pltpu.VMEM((piece_rows + SHARE, width), b16),
            pltpu.VMEM((SHARE, width), f32),
            pltpu.VMEM((count, block_rows, TILE), f32),
            pltpu.VMEM((count, piece_rows, TILE), f32),
            pltpu.VMEM((count, block_cols, TILE), f32),
            pltpu.VMEM((count, rows_n, piece_rows, TILE), f32),
            pltpu.VMEM((count, piece_rows, TILE), f32),
            pltpu.VMEM((total, TILE), f32),
            pltpu.VMEM((total // 2, TILE), f32),
            pltpu.VMEM((rows_n, total // (2 * rows_n), TILE), f32),
            pltpu.VMEM((line_n, total // shares, TILE), f32),
            pltpu.VMEM((line_n, total // (2 * rows_n), TILE), f32),
            dma((count, 2, line_n)),
            dma((count, 2, line_n)),
            dma((count, 2 * line_n)),
            dma((count, 2 * line_n)),
            dma((count, rows_n)),
            dma((count, rows_n)),
            dma((count,)),
            dma((count,)),
            dma((count,)),
            dma((count,)),
            dma((count, most)),
            dma((count,)),
            dma((count, rows_n)),
            dma((count, line_n)),
            dma((count, line_n)),
            dma((count, rows_n)),
            dma((count,)),
        ],
        compiler_params=pltpu.CompilerParams(collective_id=0, has_side_effects=True, vmem_limit_bytes=56 << 20),
    )(pattern, panel_pattern, inverse, panel, factor)
    return pl.pallas_call(
        functools.partial(write_out, chunk_rows),
        grid=(count,),
        out_shape=(jax.ShapeDtypeStruct((piece_rows, width), f32), jax.ShapeDtypeStruct((width, width), f32)),
        in_specs=[
            pl.BlockSpec((count, piece_rows, TILE), lambda i: (0, 0, 0)),
            pl.BlockSpec((total, TILE), lambda i: (0, 0)),
        ],
        out_specs=(
            pl.BlockSpec((piece_rows // count, width), lambda i: (i, 0)),
            pl.BlockSpec((TILE, width), lambda i: (i, 0)),
        ),
        compiler_params=pltpu.CompilerParams(vmem_limit_bytes=32 << 20),
    )(moved, whole)


def shards(ancestor_inverse, panel, diag_inverse, inverse_pattern, panel_pattern):
    return finish(inverse_pattern, panel_pattern, ancestor_inverse, panel, diag_inverse)


def solution(mesh):
    return jax.shard_map(
        shards,
        mesh=mesh,
        in_specs=(P("row", "col"), P(("row", "col"), None), P(), P(), P()),
        out_specs=(P(("row", "col"), None), P()),
        check_vma=False,
    )
```
